512 devices in a mesh: row: 8 (over z), col: 16 (over y, core), depth: 4 (over x).
Axes of the slice: x: 4, y: 8, z: 8, core: 2. Of those that a mesh axis runs over, the one named last changes fastest.
Arguments:
- tokens: bfloat16 [4096, 8192], P(('row', 'col'), 'depth'), may hold values from -6 to 6
- gate_weight: bfloat16 [8192, 14336], P(('depth', 'row'), 'col'), may hold values from -0.0625 to 0.0625
- up_weight: bfloat16 [8192, 14336], P(('depth', 'row'), 'col'), may hold values from -0.0625 to 0.0625
- down_weight: bfloat16 [14336, 8192], P(('col', 'row'), 'depth'), may hold values from -0.125 to 0.125
- gate_keep: int32 [64, 112], replicated, may hold values from 0 to 1, as said below
- up_keep: int32 [64, 112], replicated, may hold values from 0 to 1, as said below
- down_keep: int32 [112, 64], replicated, may hold values from 0 to 1, as said below
Outputs:
- mixed: bfloat16 [4096, 8192], P(('row', 'col'), 'depth')
The draws below stay inside these ranges and needn't reach their ends.
Inputs may be any that keep to these rules, and one draw needn't show every extreme that they name: `gate_keep`: 1 marks a kept block of the gate projection, 0 a dropped one. `up_keep`: 1 marks a kept block of the up projection, 0 a dropped one. `down_keep`: 1 marks a kept block of the down projection, 0 a dropped one.
All inputs are finite; a program needn't handle non-finite values.
Results may differ from the reference program's by a relative error of at most 0.005.
Values may be sent and summed in bfloat16 or wider, within the bound.
No kernel may reach another device: no remote copies, remote signals or barrier semaphores. Data moves between devices by JAX's collectives and lax.ppermute only.
A program may use at most 64 MiB of HBM per device.

```python
import jax
import jax.numpy as jnp

D = 8192
FF = 14336
BLOCK = 128
TOKENS = 4096


def mask_levels(key):
    return jax.random.randint(jax.random.fold_in(key, 11), (FF // BLOCK,), 1, 8)


def draw_gate_keep(key, part):
    levels = mask_levels(key)
    dice_rolls = jax.random.randint(jax.random.fold_in(key, 21), (D // BLOCK, FF // BLOCK), 0, 8)
    return (dice_rolls < levels[None, :]).astype(jnp.int32)


def draw_up_keep(key, part):
    levels = mask_levels(key)
    dice_rolls = jax.random.randint(jax.random.fold_in(key, 22), (D // BLOCK, FF // BLOCK), 0, 8)
    return (dice_rolls < levels[None, :]).astype(jnp.int32)


def draw_down_keep(key, part):
    levels = mask_levels(key)
    dice_rolls = jax.random.randint(jax.random.fold_in(key, 23), (FF // BLOCK, D // BLOCK), 0, 8)
    return (dice_rolls < levels[:, None]).astype(jnp.int32)


def level_of(own_key, shape, shards, low, high):
    def one(position, shards_of):
        draws = jax.random.uniform(jax.random.fold_in(jax.random.fold_in(own_key, 6), position), (shards_of,), jnp.float32, low / len(shards), high / len(shards))
        return jnp.repeat(jnp.exp(draws), shape[position] // shards_of).reshape((-1,) + (1,) * (len(shape) - position - 1))

    level = one(*shards[0])
    for cut in shards[1:]:
        level = level * one(*cut)
    return level


def bell_draw(rng, shape, scale, most, split=(), dtype=jnp.bfloat16):
    result = scale * jax.random.normal(rng, shape, jnp.float32)
    if split:
        result = result * level_of(rng, shape, split, -0.22, 0.18)
    return jnp.clip(result, -most, most).astype(dtype)


def setup_inputs(seed: int = 0) -> dict:
    key_list = jax.random.split(jax.random.key(seed), 8)
    return {
        "tokens": bell_draw(key_list[0], (TOKENS, D), 1.0, 6.0, ((0, 128), (1, 4))),
        "gate_weight": bell_draw(key_list[1], (D, FF), D ** -0.5, 0.0625, ((0, 32), (1, 16))),
        "up_weight": bell_draw(key_list[2], (D, FF), D ** -0.5, 0.0625, ((0, 32), (1, 16))),
        "down_weight": bell_draw(key_list[3], (FF, D), (FF // 8) ** -0.5, 0.125, ((0, 128), (1, 4))),
        "gate_keep": draw_gate_keep(jax.random.fold_in(key_list[7], 71), 0),
        "up_keep": draw_up_keep(jax.random.fold_in(key_list[7], 71), 0),
        "down_keep": draw_down_keep(jax.random.fold_in(key_list[7], 71), 0),
    }


def expand_keep(keep):
    bits = keep.astype(jnp.bfloat16)
    return jnp.repeat(jnp.repeat(bits, BLOCK, axis=0), BLOCK, axis=1)


def reference(tokens, gate_weight, up_weight, down_weight, gate_keep, up_keep, down_keep):
    gate_masked = gate_weight * expand_keep(gate_keep)
    up_masked = up_weight * expand_keep(up_keep)
    down_masked = down_weight * expand_keep(down_keep)
    gate = jnp.dot(tokens, gate_masked, preferred_element_type=jnp.float32)
    up = jnp.dot(tokens, up_masked, preferred_element_type=jnp.float32)
    hidden = (jax.nn.silu(gate) * up).astype(jnp.bfloat16)
    mixed = jnp.dot(hidden, down_masked, preferred_element_type=jnp.float32)
    return mixed.astype(jnp.bfloat16)
```

```python
import jax
import jax.numpy as jnp
from jax import lax
from jax.experimental import pallas as pl
from jax.experimental.pallas import tpu as pltpu
from jax.sharding import PartitionSpec as P

BLOCK = 128
VMEM = 56 * 1024 * 1024


def ring(size, step):
    return [(i, (i + step) % size) for i in range(size)]


def gather_ring(piece, axis):
    size = lax.axis_size(axis)
    rows = piece.shape[0]
    found = [(0, 0, piece)]
    ahead = behind = piece
    for step in range(1, size // 2):
        ahead = lax.ppermute(ahead, axis, ring(size, 1))
        behind = lax.ppermute(behind, axis, ring(size, -1))
        found += [(-step, 0, ahead), (step, 0, behind)]
    half = rows // 2
    found.append((size // 2, 0, lax.ppermute(ahead[:half], axis, ring(size, 1))))
    found.append((size // 2, half, lax.ppermute(behind[half:], axis, ring(size, -1))))
    return found


def first_kernel(offsets, up_rows, place, gate_keep, up_keep, tokens, gate, *refs):
    up_refs, out = refs[:-1], refs[-1]
    j = pl.program_id(0)
    column = place[1] + j
    gate_parts = []
    for i in range(gate.shape[0] // BLOCK):
        keep = gate_keep[place[0] + i, column].astype(jnp.bfloat16)
        gate_parts.append(gate[pl.ds(i * BLOCK, BLOCK), :] * keep)
    gate_sum = jnp.dot(tokens[...], jnp.concatenate(gate_parts, 0), preferred_element_type=jnp.float32)
    up_sum = None
    for k, ref in enumerate(up_refs):
        first = place[2 + k]
        parts = []
        for i in range(ref.shape[0] // BLOCK):
            keep = up_keep[place[0] + first + i, column].astype(jnp.bfloat16)
            parts.append(ref[pl.ds(i * BLOCK, BLOCK), :] * keep)
        masked = jnp.concatenate(parts, 0) if len(parts) > 1 else parts[0]
        left = tokens[:, pl.ds(pl.multiple_of(first * BLOCK, BLOCK), ref.shape[0])]
        term = jnp.dot(left, masked, preferred_element_type=jnp.float32)
        up_sum = term if up_sum is None else up_sum + term
    shape = out.shape[:1] + out.shape[2:]
    out[:, 0] = gate_sum.reshape(shape).astype(out.dtype)
    out[:, 1] = up_sum.reshape(shape).astype(out.dtype)


def first_product(tokens, gate, up_pieces, gate_keep, up_keep, parts, row, depth, col):
    count, features = tokens.shape
    units = gate.shape[1]
    size = lax.axis_size("row")
    rows = features // size
    place = [depth * (features // BLOCK), col * (units // BLOCK)]
    place += [((row + off) % size) * (rows // BLOCK) + start // BLOCK for off, start, _ in up_pieces]
    place = jnp.stack([jnp.asarray(p, jnp.int32) for p in place])
    arrays = [a for _, _, a in up_pieces]

    def kernel(*refs):
        first_kernel(None, None, *refs)

    return pl.pallas_call(
        kernel,
        out_shape=jax.ShapeDtypeStruct((parts, 2, count // parts, units), jnp.bfloat16),
        grid_spec=pltpu.PrefetchScalarGridSpec(
            num_scalar_prefetch=3,
            grid=(units // BLOCK,),
            in_specs=[
                pl.BlockSpec((count, features), lambda j, *_: (0, 0)),
                pl.BlockSpec((features, BLOCK), lambda j, *_: (0, j)),
            ]
            + [pl.BlockSpec((a.shape[0], BLOCK), lambda j, *_: (0, j)) for a in arrays],
            out_specs=pl.BlockSpec((parts, 2, count // parts, BLOCK), lambda j, *_: (0, 0, 0, j)),
        ),
        compiler_params=pltpu.CompilerParams(vmem_limit_bytes=VMEM),
        cost_estimate=pl.CostEstimate(
            flops=4 * count * features * units, bytes_accessed=12 * 1024 * 1024, transcendentals=0
        ),
        name="first",
    )(place, gate_keep, up_keep, tokens, gate, *arrays)


def second_kernel(place, down_keep, down, *refs):
    hidden_refs, (out_own, out_other, held) = refs[:-3], refs[-3:]
    j = pl.program_id(0)

    @pl.when(j == 0)
    def _():
        for k, ref in enumerate(hidden_refs):
            rows = ref.shape[0]
            held[pl.ds(pl.multiple_of(place[2 + k] * rows, rows), rows), :] = ref[...]

    width = down.shape[1]
    columns = []
    for n in range(width // BLOCK):
        column = place[1] + j * (width // BLOCK) + n
        parts = []
        for i in range(down.shape[0] // BLOCK):
            keep = down_keep[place[0] + i, column].astype(jnp.bfloat16)
            parts.append(down[pl.ds(i * BLOCK, BLOCK), pl.ds(n * BLOCK, BLOCK)] * keep)
        columns.append(jnp.concatenate(parts, 0))
    total = jnp.dot(held[...], jnp.concatenate(columns, 1), preferred_element_type=jnp.float32)
    half = out_own.shape[0]
    out_own[...] = total[:half].astype(out_own.dtype)
    out_other[...] = total[half:].astype(out_other.dtype)


def second_product(hidden_pieces, down, down_keep, depth, col):
    units, features = down.shape
    size = lax.axis_size("depth")
    arrays = [a for _, a in hidden_pieces]
    count = sum(a.shape[0] for a in arrays)
    width = 2 * BLOCK
    place = [col * (units // BLOCK), depth * (features // BLOCK)]
    place += [(depth + off) % size for off, _ in hidden_pieces]
    place = jnp.stack([jnp.asarray(p, jnp.int32) for p in place])
    half = jax.ShapeDtypeStruct((count // 2, features), jnp.float32)
    return pl.pallas_call(
        second_kernel,
        out_shape=(half, half),
        grid_spec=pltpu.PrefetchScalarGridSpec(
            num_scalar_prefetch=2,
            grid=(features // width,),
            in_specs=[pl.BlockSpec((units, width), lambda j, *_: (0, j))]
            + [pl.BlockSpec(a.shape, lambda j, *_: (0, 0)) for a in arrays],
            out_specs=(pl.BlockSpec((count // 2, width), lambda j, *_: (0, j)),) * 2,
            scratch_shapes=[pltpu.VMEM((count, units), jnp.bfloat16)],
        ),
        compiler_params=pltpu.CompilerParams(vmem_limit_bytes=VMEM),
        cost_estimate=pl.CostEstimate(
            flops=2 * count * features * units, bytes_accessed=9 * 1024 * 1024, transcendentals=0
        ),
        name="second",
    )(place, down_keep, down, *arrays)


def on_device(tokens, gate_weight, up_weight, down_weight, gate_keep, up_keep, down_keep):
    depth = lax.axis_index("depth")
    row = lax.axis_index("row")
    col = lax.axis_index("col")
    depth_size, col_size = lax.axis_size("depth"), lax.axis_size("col")
    ways = col_size // 2
    same_core = [list(range(c, col_size, 2)) for c in range(2)]
    swap = [(i, i ^ 1) for i in range(col_size)]

    gate = lax.all_gather(gate_weight, "row", axis=0, tiled=True)
    up_pieces = gather_ring(up_weight, "row")
    down = lax.all_gather(down_weight, "row", axis=0, tiled=True)

    spread = jnp.broadcast_to(tokens[None], (ways,) + tokens.shape)
    own = lax.all_to_all(spread, "col", 0, 0, axis_index_groups=same_core, tiled=True)
    own = own.reshape(-1, tokens.shape[1])
    other = lax.ppermute(own, "col", swap)
    token_block = jnp.concatenate([own, other], 0)

    both = first_product(
        token_block, gate, up_pieces, gate_keep, up_keep, depth_size, row, depth, col
    )
    both = lax.all_to_all(both, "depth", 0, 0, tiled=True)
    total = jnp.sum(both.astype(jnp.float32), 0)
    hidden = (jax.nn.silu(total[0]) * total[1]).astype(jnp.bfloat16)
    pieces = [(0, hidden)] + [
        (k, lax.ppermute(hidden, "depth", ring(depth_size, -k))) for k in range(1, depth_size)
    ]
    mine, theirs = second_product(pieces, down, down_keep, depth, col)
    mine = mine + lax.ppermute(theirs, "col", swap)
    mine = mine.astype(jnp.bfloat16).reshape((ways, -1, mine.shape[1]))
    mixed = lax.all_to_all(mine, "col", 0, 0, axis_index_groups=same_core, tiled=True)
    return jnp.sum(mixed.astype(jnp.float32), 0).astype(jnp.bfloat16)


def solution(mesh):
    placed = (
        P(("row", "col"), "depth"),
        P(("depth", "row"), "col"),
        P(("depth", "row"), "col"),
        P(("col", "row"), "depth"),
        P(),
        P(),
        P(),
    )
    return jax.shard_map(
        on_device, mesh=mesh, in_specs=placed, out_specs=P(("row", "col"), "depth"), check_vma=False
    )
```

```python
import functools
import math

import jax
import jax.numpy as jnp
from jax import lax
from jax.experimental import pallas as pl
from jax.experimental.pallas import tpu as pltpu
from jax.sharding import PartitionSpec as P

BLOCK = 128
VMEM = 58 * 1024 * 1024
SECOND_VMEM = 32 * 1024 * 1024
IN_VMEM = pl.BlockSpec(memory_space=pltpu.VMEM)
ANYWHERE = pl.BlockSpec(memory_space=pl.ANY)
IN_SMEM = pl.BlockSpec(memory_space=pltpu.SMEM)


def ring(size, step):
    return [(i, (i + step) % size) for i in range(size)]


def after(value, *others):
    return lax.optimization_barrier((value,) + others)[0]


def mask_kernel(step, place, keep_ref, weight, out):
    for i in range(weight.shape[0] // step):
        block = lax.div(place[0] + i * step, BLOCK)
        for n in range(weight.shape[1] // BLOCK):
            keep = keep_ref[block, place[1] + n].astype(weight.dtype)
            spot = (pl.ds(i * step, step), pl.ds(n * BLOCK, BLOCK))
            out[spot] = weight[spot] * keep


def masked(weight, keep, first_row, first_block_column):
    step = math.gcd(weight.shape[0], BLOCK)
    place = jnp.stack([first_row, first_block_column]).astype(jnp.int32)
    return pl.pallas_call(
        functools.partial(mask_kernel, step),
        out_shape=jax.ShapeDtypeStruct(weight.shape, weight.dtype),
        in_specs=[IN_SMEM, IN_SMEM, IN_VMEM],
        out_specs=IN_VMEM,
        compiler_params=pltpu.CompilerParams(vmem_limit_bytes=VMEM),
        cost_estimate=pl.CostEstimate(flops=weight.size, bytes_accessed=4 * weight.size, transcendentals=0),
        name="mask",
    )(place, keep, weight)


def product_kernel(count, added, place, gate_keep, up_keep, tokens, *refs):
    so_far = refs[0] if added else None
    pieces = refs[1 if added else 0 : -3]
    out, held, sems = refs[-3:]
    units = pieces[0].shape[1]
    copies, row = [], 0
    for k in range(count):
        rows = pieces[k].shape[0]
        for side in range(2):
            spot = (pl.ds(row, rows), pl.ds(side * units, units))
            copy = pltpu.make_async_copy(pieces[side * count + k], held.at[spot], sems.at[2 * k + side])
            copy.start()
            copies.append((row, rows, copy))
        row += rows
    firsts = [place[2 + k] for k in range(count)]
    spots = [pl.ds(pl.multiple_of(firsts[k], BLOCK), copies[2 * k][1]) for k in range(count)]
    for k, (row, rows, copy) in enumerate(copies):
        copy.wait()
        keep, left = ((gate_keep, 0), (up_keep, units))[k % 2]
        block_row = place[0] + lax.div(firsts[k // 2], BLOCK)
        for i in range(rows // BLOCK):
            for n in range(units // BLOCK):
                spot = (pl.ds(row + i * BLOCK, BLOCK), pl.ds(left + n * BLOCK, BLOCK))
                held[spot] = held[spot] * keep[block_row + i, place[1] + n].astype(held.dtype)
    half, width = tokens.shape[0] // 2, 4 * BLOCK
    for start in range(0, 2 * units, width):
        columns = pl.ds(start, min(width, 2 * units - start))
        for t in range(2):
            part = pl.ds(t * half, half)
            left = [tokens[part, spot] for spot in spots]
            left = jnp.concatenate(left, 1) if count > 1 else left[0]
            total = jnp.dot(left, held[:, columns], preferred_element_type=jnp.float32)
            if added:
                total = total + so_far[part, columns]
            out[part, columns] = total.astype(out.dtype)


def product(tokens, gates, ups, gate_keep, up_keep, so_far, dtype, name):
    row, size = lax.axis_index("row"), lax.axis_size("row")
    count, features = tokens.shape
    units = ups[0][2].shape[1]
    rows = sum(a.shape[0] for _, _, a in ups)
    place = [lax.axis_index("depth") * (features // BLOCK), lax.axis_index("col") * (units // BLOCK)]
    place += [lax.rem(row + off + size, size) * (features // size) + start for off, start, _ in ups]
    arrays = [a for _, _, a in gates] + [a for _, _, a in ups]
    added = [] if so_far is None else [so_far]
    return pl.pallas_call(
        functools.partial(product_kernel, len(ups), so_far is not None),
        out_shape=jax.ShapeDtypeStruct((count, 2 * units), dtype),
        in_specs=[IN_SMEM] * 3 + [IN_VMEM] * (1 + len(added)) + [ANYWHERE] * len(arrays),
        out_specs=IN_VMEM,
        scratch_shapes=[
            pltpu.VMEM((rows, 2 * units), jnp.bfloat16),
            pltpu.SemaphoreType.DMA((len(arrays),)),
        ],
        compiler_params=pltpu.CompilerParams(vmem_limit_bytes=VMEM),
        cost_estimate=pl.CostEstimate(
            flops=4 * count * rows * units, bytes_accessed=4 * rows * units, transcendentals=0
        ),
        name=name,
    )(jnp.stack(place).astype(jnp.int32), gate_keep, up_keep, tokens, *added, *arrays)


def second_kernel(share, place, hidden, down, out_own, out_other, held, weight, sems):
    width = down.shape[1] // sems.shape[0]
    copies = []
    for j in range(sems.shape[0]):
        columns = pl.ds(j * width, width)
        copies.append(pltpu.make_async_copy(down.at[:, columns], weight.at[:, columns], sems.at[j]))
        copies[j].start()
    half = out_own.shape[0]
    for y in range(half // share):
        for core in range(2):
            spot = lax.rem(core + place[0], 2) * half + y * share
            held[pl.ds(pl.multiple_of(spot, share), share), :] = hidden[pl.ds((2 * y + core) * share, share), :]
    for j, copy in enumerate(copies):
        copy.wait()
        columns = pl.ds(j * width, width)
        for t, out in enumerate((out_own, out_other)):
            out[:, columns] = jnp.dot(
                held[pl.ds(t * half, half), :], weight[:, columns], preferred_element_type=jnp.float32
            )


def second_product(hidden, down, share):
    count = hidden.shape[0]
    units, features = down.shape
    core = lax.rem(lax.axis_index("col"), 2).reshape((1,)).astype(jnp.int32)
    half = jax.ShapeDtypeStruct((count // 2, features), jnp.float32)
    return pl.pallas_call(
        functools.partial(second_kernel, share),
        out_shape=(half, half),
        in_specs=[IN_SMEM, IN_VMEM, ANYWHERE],
        out_specs=(IN_VMEM, IN_VMEM),
        scratch_shapes=[
            pltpu.VMEM((count, units), jnp.bfloat16),
            pltpu.VMEM((units, features), jnp.bfloat16),
            pltpu.SemaphoreType.DMA((4,)),
        ],
        compiler_params=pltpu.CompilerParams(vmem_limit_bytes=SECOND_VMEM),
        cost_estimate=pl.CostEstimate(
            flops=2 * count * features * units, bytes_accessed=9 * 1024 * 1024, transcendentals=0
        ),
        name="second",
    )(core, hidden, down)


def gather_ring(piece, axis, way):
    size = lax.axis_size(axis)
    found = [(0, 0, piece)]
    ahead = behind = piece
    for step in range(1, size // 2):
        ahead = lax.ppermute(ahead, axis, ring(size, 1))
        behind = lax.ppermute(behind, axis, ring(size, -1))
        found += [(-step, 0, ahead), (step, 0, behind)]
    found.append((size // 2, 0, lax.ppermute(ahead if way > 0 else behind, axis, ring(size, way))))
    return found


def on_device(tokens, gate_weight, up_weight, down_weight, gate_keep, up_keep, down_keep):
    depth = lax.axis_index("depth")
    row = lax.axis_index("row")
    col = lax.axis_index("col")
    depth_size, row_size, col_size = lax.axis_size("depth"), lax.axis_size("row"), lax.axis_size("col")
    same_core = [list(range(c, col_size, 2)) for c in range(2)]
    swap = [(i, i ^ 1) for i in range(col_size)]
    units = gate_weight.shape[1]

    token_block = lax.all_gather(tokens, "col", axis=0, tiled=True)
    gates, ups = gather_ring(gate_weight, "row", 1), gather_ring(up_weight, "row", -1)
    down_row = (col * row_size + row) * down_weight.shape[0]
    down = masked(down_weight, down_keep, down_row, depth * (down_weight.shape[1] // BLOCK))
    down = after(down, *[a for _, _, a in gates[-3:-1] + ups[-3:-1]])
    down = lax.all_gather(down, "row", axis=0, tiled=True)

    so_far = product(token_block, gates[:-1], ups[:-1], gate_keep, up_keep, None, jnp.float32, "most")
    gate, up, so_far = lax.optimization_barrier((gates[-1][2], ups[-1][2], so_far))
    both = product(
        token_block,
        [gates[-1][:2] + (gate,)],
        [ups[-1][:2] + (up,)],
        gate_keep,
        up_keep,
        so_far,
        jnp.bfloat16,
        "last",
    )
    both = both.reshape((depth_size, -1, both.shape[1]))
    both = lax.all_to_all(both, "depth", 0, 0, tiled=True)
    both = jnp.sum(both.astype(jnp.float32), 0)
    hidden = (jax.nn.silu(both[:, :units]) * both[:, units:]).astype(jnp.bfloat16)
    hidden = lax.all_gather(hidden, "depth", axis=0, tiled=True)

    mine, theirs = second_product(hidden, down, tokens.shape[0])
    mine = mine + lax.ppermute(theirs, "col", swap)
    mine = mine.astype(jnp.bfloat16).reshape((col_size // 2,) + tokens.shape)
    mixed = lax.all_to_all(mine, "col", 0, 0, axis_index_groups=same_core, tiled=True)
    return jnp.sum(mixed.astype(jnp.float32), 0).astype(jnp.bfloat16)


def solution(mesh):
    placed = (
        P(("row", "col"), "depth"),
        P(("depth", "row"), "col"),
        P(("depth", "row"), "col"),
        P(("col", "row"), "depth"),
        P(),
        P(),
        P(),
    )
    return jax.shard_map(
        on_device, mesh=mesh, in_specs=placed, out_specs=P(("row", "col"), "depth"), check_vma=False
    )
```

```python
import functools
import math

import jax
import jax.numpy as jnp
from jax import lax
from jax.experimental import pallas as pl
from jax.experimental.pallas import tpu as pltpu
from jax.sharding import PartitionSpec as P

BLOCK = 128
VMEM = 58 * 1024 * 1024
SECOND_VMEM = 32 * 1024 * 1024
IN_VMEM = pl.BlockSpec(memory_space=pltpu.VMEM)
ANYWHERE = pl.BlockSpec(memory_space=pl.ANY)
IN_SMEM = pl.BlockSpec(memory_space=pltpu.SMEM)


def ring(size, step):
    return [(i, (i + step) % size) for i in range(size)]


def after(value, *others):
    return lax.optimization_barrier((value,) + others)[0]


def mask_kernel(step, place, keep_ref, weight, out):
    for i in range(weight.shape[0] // step):
        block = lax.div(place[0] + i * step, BLOCK)
        for n in range(weight.shape[1] // BLOCK):
            keep = keep_ref[block, place[1] + n].astype(weight.dtype)
            spot = (pl.ds(i * step, step), pl.ds(n * BLOCK, BLOCK))
            out[spot] = weight[spot] * keep


def masked(weight, keep, first_row, first_block_column):
    step = math.gcd(weight.shape[0], BLOCK)
    place = jnp.stack([first_row, first_block_column]).astype(jnp.int32)
    return pl.pallas_call(
        functools.partial(mask_kernel, step),
        out_shape=jax.ShapeDtypeStruct(weight.shape, weight.dtype),
        in_specs=[IN_SMEM, IN_SMEM, IN_VMEM],
        out_specs=IN_VMEM,
        compiler_params=pltpu.CompilerParams(vmem_limit_bytes=VMEM),
        cost_estimate=pl.CostEstimate(flops=weight.size, bytes_accessed=4 * weight.size, transcendentals=0),
        name="mask",
    )(place, keep, weight)


def product_kernel(place, keep_ref, tokens, *refs):
    pieces = refs[:-3]
    out, held, sems = refs[-3:]
    units = held.shape[1]
    copies, row = [], 0
    for k, ref in enumerate(pieces):
        copy = pltpu.make_async_copy(ref, held.at[pl.ds(row, ref.shape[0]), :], sems.at[k])
        copy.start()
        copies.append((row, ref.shape[0], copy))
        row += ref.shape[0]
    firsts = [place[2 + k] for k in range(len(pieces))]
    spots = [pl.ds(pl.multiple_of(first, BLOCK), rows) for first, (_, rows, _) in zip(firsts, copies)]
    for first, (row, rows, copy) in zip(firsts, copies):
        copy.wait()
        block_row = place[0] + lax.div(first, BLOCK)
        for i in range(rows // BLOCK):
            for n in range(units // BLOCK):
                spot = (pl.ds(row + i * BLOCK, BLOCK), pl.ds(n * BLOCK, BLOCK))
                held[spot] = held[spot] * keep_ref[block_row + i, place[1] + n].astype(held.dtype)
    half, width = tokens.shape[0] // 2, 4 * BLOCK
    for start in range(0, units, width):
        columns = pl.ds(start, min(width, units - start))
        for t in range(2):
            part = pl.ds(t * half, half)
            left = jnp.concatenate([tokens[part, spot] for spot in spots], 1)
            total = jnp.dot(left, held[:, columns], preferred_element_type=jnp.float32)
            out[part, columns] = total.astype(out.dtype)


def product(tokens, pieces, keep, name):
    row, size = lax.axis_index("row"), lax.axis_size("row")
    count, features = tokens.shape
    units = pieces[0][1].shape[1]
    place = [lax.axis_index("depth") * (features // BLOCK), lax.axis_index("col") * (units // BLOCK)]
    place += [lax.rem(row + off + size, size) * (features // size) for off, _ in pieces]
    arrays = [a for _, a in pieces]
    return pl.pallas_call(
        product_kernel,
        out_shape=jax.ShapeDtypeStruct((count, units), jnp.bfloat16),
        in_specs=[IN_SMEM] * 2 + [IN_VMEM] + [ANYWHERE] * len(arrays),
        out_specs=IN_VMEM,
        scratch_shapes=[
            pltpu.VMEM((features, units), jnp.bfloat16),
            pltpu.SemaphoreType.DMA((len(arrays),)),
        ],
        compiler_params=pltpu.CompilerParams(vmem_limit_bytes=VMEM),
        cost_estimate=pl.CostEstimate(
            flops=2 * count * features * units, bytes_accessed=2 * features * units, transcendentals=0
        ),
        name=name,
    )(jnp.stack(place).astype(jnp.int32), keep, tokens, *arrays)


def second_kernel(share, place, hidden, down, out_own, out_other, held, weight, sems):
    width = down.shape[1] // sems.shape[0]
    copies = []
    for j in range(sems.shape[0]):
        columns = pl.ds(j * width, width)
        copies.append(pltpu.make_async_copy(down.at[:, columns], weight.at[:, columns], sems.at[j]))
        copies[j].start()
    half = out_own.shape[0]
    for y in range(half // share):
        for core in range(2):
            spot = lax.rem(core + place[0], 2) * half + y * share
            held[pl.ds(pl.multiple_of(spot, share), share), :] = hidden[pl.ds((2 * y + core) * share, share), :]
    for j, copy in enumerate(copies):
        copy.wait()
        columns = pl.ds(j * width, width)
        for t, out in enumerate((out_own, out_other)):
            out[:, columns] = jnp.dot(
                held[pl.ds(t * half, half), :], weight[:, columns], preferred_element_type=jnp.float32
            )


def second_product(hidden, down, share):
    count = hidden.shape[0]
    units, features = down.shape
    core = lax.rem(lax.axis_index("col"), 2).reshape((1,)).astype(jnp.int32)
    half = jax.ShapeDtypeStruct((count // 2, features), jnp.float32)
    return pl.pallas_call(
        functools.partial(second_kernel, share),
        out_shape=(half, half),
        in_specs=[IN_SMEM, IN_VMEM, ANYWHERE],
        out_specs=(IN_VMEM, IN_VMEM),
        scratch_shapes=[
            pltpu.VMEM((count, units), jnp.bfloat16),
            pltpu.VMEM((units, features), jnp.bfloat16),
            pltpu.SemaphoreType.DMA((4,)),
        ],
        compiler_params=pltpu.CompilerParams(vmem_limit_bytes=SECOND_VMEM),
        cost_estimate=pl.CostEstimate(
            flops=2 * count * features * units, bytes_accessed=9 * 1024 * 1024, transcendentals=0
        ),
        name="second",
    )(core, hidden, down)


def gather_ring(piece, axis, way):
    size = lax.axis_size(axis)
    found = [(0, piece)]
    ahead = behind = piece
    for step in range(1, size // 2):
        ahead = lax.ppermute(ahead, axis, ring(size, 1))
        behind = lax.ppermute(behind, axis, ring(size, -1))
        found += [(-step, ahead), (step, behind)]
    found.append((size // 2, lax.ppermute(ahead if way > 0 else behind, axis, ring(size, way))))
    return found


def on_device(tokens, gate_weight, up_weight, down_weight, gate_keep, up_keep, down_keep):
    depth = lax.axis_index("depth")
    row = lax.axis_index("row")
    col = lax.axis_index("col")
    depth_size, row_size, col_size = lax.axis_size("depth"), lax.axis_size("row"), lax.axis_size("col")
    same_core = [list(range(c, col_size, 2)) for c in range(2)]
    swap = [(i, i ^ 1) for i in range(col_size)]
    units = gate_weight.shape[1]

    token_block = lax.all_gather(tokens, "col", axis=0, tiled=True)
    gates, ups = gather_ring(gate_weight, "row", 1), gather_ring(up_weight, "row", -1)
    down_row = (col * row_size + row) * down_weight.shape[0]
    down = masked(down_weight, down_keep, down_row, depth * (down_weight.shape[1] // BLOCK))
    down = after(down, *[a for _, a in gates[-3:] + ups[-3:-1]])
    down = lax.all_gather(down, "row", axis=0, tiled=True)

    def exchange(share):
        return lax.all_to_all(share.reshape((depth_size, -1, units)), "depth", 0, 0, tiled=True)

    gate = product(token_block, gates, gate_keep, "gate")
    last, gate = lax.optimization_barrier((ups[-1][1], gate))
    gate = exchange(gate)
    up = product(token_block, ups[:-1] + [(ups[-1][0], last)], up_keep, "up")
    up, gate = lax.optimization_barrier((up, gate))
    up = exchange(up)
    gate, up = [jnp.sum(share.astype(jnp.float32), 0) for share in (gate, up)]
    hidden = (jax.nn.silu(gate) * up).astype(jnp.bfloat16)
    hidden = lax.all_gather(hidden, "depth", axis=0, tiled=True)

    mine, theirs = second_product(hidden, down, tokens.shape[0])
    mine = mine + lax.ppermute(theirs, "col", swap)
    mine = mine.astype(jnp.bfloat16).reshape((col_size // 2,) + tokens.shape)
    mixed = lax.all_to_all(mine, "col", 0, 0, axis_index_groups=same_core, tiled=True)
    return jnp.sum(mixed.astype(jnp.float32), 0).astype(jnp.bfloat16)


def solution(mesh):
    placed = (
        P(("row", "col"), "depth"),
        P(("depth", "row"), "col"),
        P(("depth", "row"), "col"),
        P(("col", "row"), "depth"),
        P(),
        P(),
        P(),
    )
    return jax.shard_map(
        on_device, mesh=mesh, in_specs=placed, out_specs=P(("row", "col"), "depth"), check_vma=False
    )
```

```python
import functools
import math

import jax
import jax.numpy as jnp
from jax import lax
from jax.experimental import pallas as pl
from jax.experimental.pallas import tpu as pltpu
from jax.sharding import PartitionSpec as P

BLOCK = 128
VMEM = 58 * 1024 * 1024
SECOND_VMEM = 32 * 1024 * 1024
IN_VMEM = pl.BlockSpec(memory_space=pltpu.VMEM)
ANYWHERE = pl.BlockSpec(memory_space=pl.ANY)
IN_SMEM = pl.BlockSpec(memory_space=pltpu.SMEM)


def ring(size, step):
    return [(i, (i + step) % size) for i in range(size)]


def after(value, *others):
    return lax.optimization_barrier((value,) + others)[0]


def mask_kernel(step, place, keep_ref, weight, out):
    for i in range(weight.shape[0] // step):
        block = lax.div(place[0] + i * step, BLOCK)
        for n in range(weight.shape[1] // BLOCK):
            keep = keep_ref[block, place[1] + n].astype(weight.dtype)
            spot = (pl.ds(i * step, step), pl.ds(n * BLOCK, BLOCK))
            out[spot] = weight[spot] * keep


def masked(weight, keep, first_row, first_block_column):
    step = math.gcd(weight.shape[0], BLOCK)
    place = jnp.stack([first_row, first_block_column]).astype(jnp.int32)
    return pl.pallas_call(
        functools.partial(mask_kernel, step),
        out_shape=jax.ShapeDtypeStruct(weight.shape, weight.dtype),
        in_specs=[IN_SMEM, IN_SMEM, IN_VMEM],
        out_specs=IN_VMEM,
        compiler_params=pltpu.CompilerParams(vmem_limit_bytes=VMEM),
        cost_estimate=pl.CostEstimate(flops=weight.size, bytes_accessed=4 * weight.size, transcendentals=0),
        name="mask",
    )(place, keep, weight)


def product_kernel(place, keep_ref, tokens, *refs):
    pieces = refs[:-3]
    out, held, sems = refs[-3:]
    units = held.shape[1]
    copies, row = [], 0
    for k, ref in enumerate(pieces):
        copy = pltpu.make_async_copy(ref, held.at[pl.ds(row, ref.shape[0]), :], sems.at[k])
        copy.start()
        copies.append((row, ref.shape[0], copy))
        row += ref.shape[0]
    firsts = [place[2 + k] for k in range(len(pieces))]
    spots = [pl.ds(pl.multiple_of(first, BLOCK), rows) for first, (_, rows, _) in zip(firsts, copies)]
    for first, (row, rows, copy) in zip(firsts, copies):
        copy.wait()
        block_row = place[0] + lax.div(first, BLOCK)
        for i in range(rows // BLOCK):
            for n in range(units // BLOCK):
                spot = (pl.ds(row + i * BLOCK, BLOCK), pl.ds(n * BLOCK, BLOCK))
                held[spot] = held[spot] * keep_ref[block_row + i, place[1] + n].astype(held.dtype)
    half, width = tokens.shape[0] // 2, 4 * BLOCK
    for start in range(0, units, width):
        columns = pl.ds(start, min(width, units - start))
        for t in range(2):
            part = pl.ds(t * half, half)
            left = jnp.concatenate([tokens[part, spot] for spot in spots], 1)
            total = jnp.dot(left, held[:, columns], preferred_element_type=jnp.float32)
            out[part, columns] = total.astype(out.dtype)


def product(tokens, pieces, keep, name):
    row, size = lax.axis_index("row"), lax.axis_size("row")
    count, features = tokens.shape
    units = pieces[0][1].shape[1]
    place = [lax.axis_index("depth") * (features // BLOCK), lax.axis_index("col") * (units // BLOCK)]
    place += [lax.rem(row + off + size, size) * (features // size) for off, _ in pieces]
    arrays = [a for _, a in pieces]
    return pl.pallas_call(
        product_kernel,
        out_shape=jax.ShapeDtypeStruct((count, units), jnp.bfloat16),
        in_specs=[IN_SMEM] * 2 + [IN_VMEM] + [ANYWHERE] * len(arrays),
        out_specs=IN_VMEM,
        scratch_shapes=[
            pltpu.VMEM((features, units), jnp.bfloat16),
            pltpu.SemaphoreType.DMA((len(arrays),)),
        ],
        compiler_params=pltpu.CompilerParams(vmem_limit_bytes=VMEM),
        cost_estimate=pl.CostEstimate(
            flops=2 * count * features * units, bytes_accessed=2 * features * units, transcendentals=0
        ),
        name=name,
    )(jnp.stack(place).astype(jnp.int32), keep, tokens, *arrays)


def second_kernel(share, side, place, hidden, down, out, held, weight, sems):
    width = down.shape[1] // sems.shape[0]
    copies = []
    for j in range(sems.shape[0]):
        columns = pl.ds(j * width, width)
        copies.append(pltpu.make_async_copy(down.at[:, columns], weight.at[:, columns], sems.at[j]))
        copies[j].start()
    core = lax.rem(place[0] + side, 2)
    for y in range(out.shape[0] // share):
        spot = pl.multiple_of((2 * y + core) * share, share)
        held[pl.ds(y * share, share), :] = hidden[pl.ds(spot, share), :]
    for j, copy in enumerate(copies):
        copy.wait()
        columns = pl.ds(j * width, width)
        out[:, columns] = jnp.dot(held[...], weight[:, columns], preferred_element_type=jnp.float32)


def second_product(hidden, down, share, side):
    count = hidden.shape[0]
    units, features = down.shape
    core = lax.rem(lax.axis_index("col"), 2).reshape((1,)).astype(jnp.int32)
    return pl.pallas_call(
        functools.partial(second_kernel, share, side),
        out_shape=jax.ShapeDtypeStruct((count // 2, features), jnp.float32),
        in_specs=[IN_SMEM, IN_VMEM, ANYWHERE],
        out_specs=IN_VMEM,
        scratch_shapes=[
            pltpu.VMEM((count // 2, units), jnp.bfloat16),
            pltpu.VMEM((units, features), jnp.bfloat16),
            pltpu.SemaphoreType.DMA((4,)),
        ],
        compiler_params=pltpu.CompilerParams(vmem_limit_bytes=SECOND_VMEM),
        cost_estimate=pl.CostEstimate(
            flops=count * features * units, bytes_accessed=6 * 1024 * 1024, transcendentals=0
        ),
        name="second",
    )(core, hidden, down)


def gather_ring(piece, axis, way):
    size = lax.axis_size(axis)
    found = [(0, piece)]
    ahead = behind = piece
    for step in range(1, size // 2):
        ahead = lax.ppermute(ahead, axis, ring(size, 1))
        behind = lax.ppermute(behind, axis, ring(size, -1))
        found += [(-step, ahead), (step, behind)]
    found.append((size // 2, lax.ppermute(ahead if way > 0 else behind, axis, ring(size, way))))
    return found


def on_device(tokens, gate_weight, up_weight, down_weight, gate_keep, up_keep, down_keep):
    depth = lax.axis_index("depth")
    row = lax.axis_index("row")
    col = lax.axis_index("col")
    depth_size, row_size, col_size = lax.axis_size("depth"), lax.axis_size("row"), lax.axis_size("col")
    same_core = [list(range(c, col_size, 2)) for c in range(2)]
    swap = [(i, i ^ 1) for i in range(col_size)]
    units = gate_weight.shape[1]

    token_block = lax.all_gather(tokens, "col", axis=0, tiled=True)
    gates, ups = gather_ring(gate_weight, "row", 1), gather_ring(up_weight, "row", -1)
    down_row = (col * row_size + row) * down_weight.shape[0]
    down = masked(down_weight, down_keep, down_row, depth * (down_weight.shape[1] // BLOCK))
    down = after(down, *[a for _, a in gates[-3:] + ups[-3:-1]])
    down = lax.all_gather(down, "row", axis=0, tiled=True)

    def exchange(share):
        return lax.all_to_all(share.reshape((depth_size, -1, units)), "depth", 0, 0, tiled=True)

    gate = product(token_block, gates, gate_keep, "gate")
    last, gate = lax.optimization_barrier((ups[-1][1], gate))
    gate = exchange(gate)
    up = product(token_block, ups[:-1] + [(ups[-1][0], last)], up_keep, "up")
    up, gate = lax.optimization_barrier((up, gate))
    up = exchange(up)
    gate, up = [jnp.sum(share.astype(jnp.float32), 0) for share in (gate, up)]
    hidden = (jax.nn.silu(gate) * up).astype(jnp.bfloat16)
    hidden = lax.all_gather(hidden, "depth", axis=0, tiled=True)

    theirs = lax.ppermute(second_product(hidden, down, tokens.shape[0], 1), "col", swap)
    mine = second_product(hidden, down, tokens.shape[0], 0) + theirs
    mine = mine.astype(jnp.bfloat16).reshape((col_size // 2,) + tokens.shape)
    mixed = lax.all_to_all(mine, "col", 0, 0, axis_index_groups=same_core, tiled=True)
    return jnp.sum(mixed.astype(jnp.float32), 0).astype(jnp.bfloat16)


def solution(mesh):
    placed = (
        P(("row", "col"), "depth"),
        P(("depth", "row"), "col"),
        P(("depth", "row"), "col"),
        P(("col", "row"), "depth"),
        P(),
        P(),
        P(),
    )
    return jax.shard_map(
        on_device, mesh=mesh, in_specs=placed, out_specs=P(("row", "col"), "depth"), check_vma=False
    )
```

```python
import functools
import math

import jax
import jax.numpy as jnp
from jax import lax
from jax.experimental import pallas as pl
from jax.experimental.pallas import tpu as pltpu
from jax.sharding import PartitionSpec as P

BLOCK = 128
VMEM = 58 * 1024 * 1024
SECOND_VMEM = 32 * 1024 * 1024
IN_VMEM = pl.BlockSpec(memory_space=pltpu.VMEM)
ANYWHERE = pl.BlockSpec(memory_space=pl.ANY)
IN_SMEM = pl.BlockSpec(memory_space=pltpu.SMEM)


def ring(size, step):
    return [(i, (i + step) % size) for i in range(size)]


def after(value, *others):
    return lax.optimization_barrier((value,) + others)[0]


def mask_kernel(step, place, keep_ref, weight, out):
    for i in range(weight.shape[0] // step):
        block = lax.div(place[0] + i * step, BLOCK)
        for n in range(weight.shape[1] // BLOCK):
            keep = keep_ref[block, place[1] + n].astype(weight.dtype)
            spot = (pl.ds(i * step, step), pl.ds(n * BLOCK, BLOCK))
            out[spot] = weight[spot] * keep


def masked(weight, keep, first_row, first_block_column):
    step = math.gcd(weight.shape[0], BLOCK)
    place = jnp.stack([first_row, first_block_column]).astype(jnp.int32)
    return pl.pallas_call(
        functools.partial(mask_kernel, step),
        out_shape=jax.ShapeDtypeStruct(weight.shape, weight.dtype),
        in_specs=[IN_SMEM, IN_SMEM, IN_VMEM],
        out_specs=IN_VMEM,
        compiler_params=pltpu.CompilerParams(vmem_limit_bytes=VMEM),
        cost_estimate=pl.CostEstimate(flops=weight.size, bytes_accessed=4 * weight.size, transcendentals=0),
        name="mask",
    )(place, keep, weight)


def product_kernel(place, keep_ref, tokens, *refs):
    pieces = refs[:-3]
    out, held, sems = refs[-3:]
    units = held.shape[1]
    copies, row = [], 0
    for k, ref in enumerate(pieces):
        copy = pltpu.make_async_copy(ref, held.at[pl.ds(row, ref.shape[0]), :], sems.at[k])
        copy.start()
        copies.append((row, ref.shape[0], copy))
        row += ref.shape[0]
    firsts = [place[2 + k] for k in range(len(pieces))]
    spots = [pl.ds(pl.multiple_of(first, BLOCK), rows) for first, (_, rows, _) in zip(firsts, copies)]
    for first, (row, rows, copy) in zip(firsts, copies):
        copy.wait()
        block_row = place[0] + lax.div(first, BLOCK)
        for i in range(rows // BLOCK):
            for n in range(units // BLOCK):
                spot = (pl.ds(row + i * BLOCK, BLOCK), pl.ds(n * BLOCK, BLOCK))
                held[spot] = held[spot] * keep_ref[block_row + i, place[1] + n].astype(held.dtype)
    half, width = tokens.shape[0] // 2, 4 * BLOCK
    for start in range(0, units, width):
        columns = pl.ds(start, min(width, units - start))
        for t in range(2):
            part = pl.ds(t * half, half)
            left = jnp.concatenate([tokens[part, spot] for spot in spots], 1)
            total = jnp.dot(left, held[:, columns], preferred_element_type=jnp.float32)
            out[part, columns] = total.astype(out.dtype)


def product(tokens, pieces, keep, name):
    row, size = lax.axis_index("row"), lax.axis_size("row")
    count, features = tokens.shape
    units = pieces[0][1].shape[1]
    place = [lax.axis_index("depth") * (features // BLOCK), lax.axis_index("col") * (units // BLOCK)]
    place += [lax.rem(row + off + size, size) * (features // size) for off, _ in pieces]
    arrays = [a for _, a in pieces]
    return pl.pallas_call(
        product_kernel,
        out_shape=jax.ShapeDtypeStruct((count, units), jnp.bfloat16),
        in_specs=[IN_SMEM] * 2 + [IN_VMEM] + [ANYWHERE] * len(arrays),
        out_specs=IN_VMEM,
        scratch_shapes=[
            pltpu.VMEM((features, units), jnp.bfloat16),
            pltpu.SemaphoreType.DMA((len(arrays),)),
        ],
        compiler_params=pltpu.CompilerParams(vmem_limit_bytes=VMEM),
        cost_estimate=pl.CostEstimate(
            flops=2 * count * features * units, bytes_accessed=2 * features * units, transcendentals=0
        ),
        name=name,
    )(jnp.stack(place).astype(jnp.int32), keep, tokens, *arrays)


def second_kernel(share, side, place, hidden, down, out, held):
    width = 4 * BLOCK
    core = lax.rem(place[0] + side, 2)
    for y in range(out.shape[0] // share):
        spot = pl.multiple_of((2 * y + core) * share, share)
        held[pl.ds(y * share, share), :] = hidden[pl.ds(spot, share), :]
    for start in range(0, down.shape[1], width):
        columns = pl.ds(start, width)
        out[:, columns] = jnp.dot(held[...], down[:, columns], preferred_element_type=jnp.float32)


def second_product(hidden, down, share, side):
    count = hidden.shape[0]
    units, features = down.shape
    core = lax.rem(lax.axis_index("col"), 2).reshape((1,)).astype(jnp.int32)
    return pl.pallas_call(
        functools.partial(second_kernel, share, side),
        out_shape=jax.ShapeDtypeStruct((count // 2, features), jnp.float32),
        in_specs=[IN_SMEM, IN_VMEM, IN_VMEM],
        out_specs=IN_VMEM,
        scratch_shapes=[
            pltpu.VMEM((count // 2, units), jnp.bfloat16),
        ],
        compiler_params=pltpu.CompilerParams(vmem_limit_bytes=SECOND_VMEM),
        cost_estimate=pl.CostEstimate(
            flops=count * features * units, bytes_accessed=6 * 1024 * 1024, transcendentals=0
        ),
        name="second",
    )(core, hidden, down)


def gather_ring(piece, axis, way):
    size = lax.axis_size(axis)
    found = [(0, piece)]
    ahead = behind = piece
    for step in range(1, size // 2):
        ahead = lax.ppermute(ahead, axis, ring(size, 1))
        behind = lax.ppermute(behind, axis, ring(size, -1))
        found += [(-step, ahead), (step, behind)]
    found.append((size // 2, lax.ppermute(ahead if way > 0 else behind, axis, ring(size, way))))
    return found


def on_device(tokens, gate_weight, up_weight, down_weight, gate_keep, up_keep, down_keep):
    depth = lax.axis_index("depth")
    row = lax.axis_index("row")
    col = lax.axis_index("col")
    depth_size, row_size, col_size = lax.axis_size("depth"), lax.axis_size("row"), lax.axis_size("col")
    same_core = [list(range(c, col_size, 2)) for c in range(2)]
    swap = [(i, i ^ 1) for i in range(col_size)]
    units = gate_weight.shape[1]

    token_block = lax.all_gather(tokens, "col", axis=0, tiled=True)
    gates, ups = gather_ring(gate_weight, "row", 1), gather_ring(up_weight, "row", -1)
    down_row = (col * row_size + row) * down_weight.shape[0]
    down = masked(down_weight, down_keep, down_row, depth * (down_weight.shape[1] // BLOCK))
    down = after(down, *[a for _, a in gates[-3:] + ups[-3:-1]])
    down = lax.all_gather(down, "row", axis=0, tiled=True)

    def exchange(share):
        return lax.all_to_all(share.reshape((depth_size, -1, units)), "depth", 0, 0, tiled=True)

    gate = product(token_block, gates, gate_keep, "gate")
    last, gate = lax.optimization_barrier((ups[-1][1], gate))
    gate = exchange(gate)
    up = product(token_block, ups[:-1] + [(ups[-1][0], last)], up_keep, "up")
    up, gate = lax.optimization_barrier((up, gate))
    up = exchange(up)
    gate, up = [jnp.sum(share.astype(jnp.float32), 0) for share in (gate, up)]
    hidden = (jax.nn.silu(gate) * up).astype(jnp.bfloat16)
    hidden = lax.all_gather(hidden, "depth", axis=0, tiled=True)

    theirs = lax.ppermute(second_product(hidden, down, tokens.shape[0], 1), "col", swap)
    mine = second_product(hidden, down, tokens.shape[0], 0) + theirs
    mine = mine.astype(jnp.bfloat16).reshape((col_size // 2,) + tokens.shape)
    mixed = lax.all_to_all(mine, "col", 0, 0, axis_index_groups=same_core, tiled=True)
    return jnp.sum(mixed.astype(jnp.float32), 0).astype(jnp.bfloat16)


def solution(mesh):
    placed = (
        P(("row", "col"), "depth"),
        P(("depth", "row"), "col"),
        P(("depth", "row"), "col"),
        P(("col", "row"), "depth"),
        P(),
        P(),
        P(),
    )
    return jax.shard_map(
        on_device, mesh=mesh, in_specs=placed, out_specs=P(("row", "col"), "depth"), check_vma=False
    )
```
